256 devices in a mesh: section: 8 (over x, core), tensor: 32 (over z, y).
Axes of the slice: x: 4, y: 4, z: 8, core: 2. Of those that a mesh axis runs over, the one named last changes fastest.
Arguments:
- layer_input: bfloat16 [8, 256, 8192], P('section', None, 'tensor'), may hold values from -6 to 6
- upstream: bfloat16 [8, 256, 8192], P('section', None, 'tensor'), may hold values from -6 to 6
- query_rows: bfloat16 [8, 256, 8192], P('section', None, 'tensor'), may hold values from -4.5 to 4.5
- key_rows: bfloat16 [8, 256, 8192], P('section', None, 'tensor'), may hold values from -4.5 to 4.5
- norm_gain: bfloat16 [8, 8192], P('section'), may hold values from 0.5 to 1.5
- out_tiles: bfloat16 [8, 10240, 4096], P('section', 'tensor'), may hold values from -0.09375 to 0.09375
- out_ids: int32 [8, 10240], P('section', 'tensor'), may hold values from 0 to 511, as said below
- out_count: int32 [8, 32], P('section', 'tensor'), may hold values from 192 to 320, as said below
- value_tiles: bfloat16 [8, 10240, 4096], P('section', 'tensor'), may hold values from -0.09375 to 0.09375
- value_ids: int32 [8, 10240], P('section', 'tensor'), may hold values from 0 to 511, as said below
- value_count: int32 [8, 32], P('section', 'tensor'), may hold values from 192 to 320, as said below
Outputs:
- grad_input: bfloat16 [8, 256, 8192], P('section', None, 'tensor')
- out_grad: bfloat16 [8, 10240, 4096], P('section', 'tensor')
- value_grad: bfloat16 [8, 10240, 4096], P('section', 'tensor')
The draws below stay inside these ranges and needn't reach their ends.
Inputs may be any that keep to these rules, and one draw needn't show every extreme that they name: `out_ids`: within each shard's 320 slots the tile numbers are distinct; slots at or after the shard's count are not stored tiles. `out_count`: in every section some shard holds exactly 320 stored tiles. `value_ids`: within each shard's 320 slots the tile numbers are distinct; slots at or after the shard's count are not stored tiles. `value_count`: in every section some shard holds exactly 320 stored tiles.
All inputs are finite; a program needn't handle non-finite values.
Results may differ from the reference program's by a relative error of at most 0.0085.
Values may be sent and summed in bfloat16 or wider, within the bound.
A program may use at most 128 MiB of HBM per device.

```python
import jax
import jax.numpy as jnp
from jax import lax

D = 8192
HEAD = 128
EDGE = 64
TOK = 256
SECTIONS = 8
SHARDS = 32
LOCAL = 256
TILES = 512
CAP = 320
SLOTS = 10240


def draw_query_rows(key, part):
    key = jax.random.fold_in(key, 5)
    return jax.random.truncated_normal(key, -4.0, 4.0, (SECTIONS, TOK, D), jnp.float32).astype(jnp.bfloat16)


def draw_key_rows(key, part):
    key = jax.random.fold_in(key, 7)
    return jax.random.truncated_normal(key, -4.0, 4.0, (SECTIONS, TOK, D), jnp.float32).astype(jnp.bfloat16)


def tile_order(key):
    scores = jax.random.randint(key, (SECTIONS, SHARDS, TILES), 0, 2 ** 18) * TILES
    scores = scores + jnp.arange(TILES, dtype=jnp.int32)[None, None, :]
    order = jnp.argsort(scores, axis=-1)
    return order[:, :, :CAP].reshape(SECTIONS, SHARDS * CAP).astype(jnp.int32)


def shard_counts(key):
    first_key, second_key = jax.random.split(key)
    counts = jax.random.randint(first_key, (SECTIONS, SHARDS), 3 * TILES // 8, CAP + 1)
    fullest = jax.random.randint(second_key, (SECTIONS, 1), 0, SHARDS)
    return jnp.where(jnp.arange(SHARDS, dtype=jnp.int32)[None, :] == fullest, CAP, counts).astype(jnp.int32)


def draw_out_ids(key, part):
    key = jax.random.fold_in(key, 11)
    return tile_order(key)


def draw_out_count(key, part):
    key = jax.random.fold_in(key, 13)
    return shard_counts(key)


def draw_value_ids(key, part):
    key = jax.random.fold_in(key, 17)
    return tile_order(key)


def draw_value_count(key, part):
    key = jax.random.fold_in(key, 19)
    return shard_counts(key)


def shard_levels(key, shape, cuts, low, high):
    factor_of = 1.0
    for axis_at, parts in cuts:
        draws = jax.random.uniform(jax.random.fold_in(jax.random.fold_in(key, 6), axis_at), (parts,), jnp.float32, low / len(cuts), high / len(cuts))
        factor_of = factor_of * jnp.repeat(jnp.exp(draws), shape[axis_at] // parts).reshape((-1,) + (1,) * (len(shape) - 1 - axis_at))
    return factor_of


def centred(stream_key, shape, spread, reach, pieces=(), kind=jnp.bfloat16):
    gain = shard_levels(stream_key, shape, pieces, -0.22, 0.18) if pieces else 1.0
    array = jax.random.normal(stream_key, shape, jnp.float32) * spread * gain
    return jnp.minimum(jnp.maximum(array, -reach), reach).astype(kind)


def setup_inputs(seed: int = 0) -> dict:
    streams_of = jax.random.split(jax.random.key(seed), 12)
    layer_input = centred(streams_of[0], (SECTIONS, TOK, D), 1.0, 6.0, ((0, 8), (2, 32)))
    upstream = centred(streams_of[1], (SECTIONS, TOK, D), 1.0, 6.0, ((0, 8), (2, 32)))
    query_rows = draw_query_rows(jax.random.fold_in(streams_of[11], 71), 0)
    key_rows = draw_key_rows(jax.random.fold_in(streams_of[11], 71), 0)
    norm_gain = jnp.clip(1.0 + 0.1 * jax.random.normal(streams_of[4], (SECTIONS, D), jnp.float32), 0.5, 1.5).astype(jnp.bfloat16)
    out_tiles = centred(streams_of[5], (SECTIONS, SLOTS, EDGE * EDGE), (D // 2) ** -0.5, 0.09375, ((0, 8), (1, 32)))
    out_ids = draw_out_ids(jax.random.fold_in(streams_of[11], 71), 0)
    out_count = draw_out_count(jax.random.fold_in(streams_of[11], 71), 0)
    value_tiles = centred(streams_of[8], (SECTIONS, SLOTS, EDGE * EDGE), (D // 2) ** -0.5, 0.09375, ((0, 8), (1, 32)))
    value_ids = draw_value_ids(jax.random.fold_in(streams_of[11], 71), 0)
    value_count = draw_value_count(jax.random.fold_in(streams_of[11], 71), 0)
    return dict(layer_input=layer_input, upstream=upstream, query_rows=query_rows, key_rows=key_rows, norm_gain=norm_gain, out_tiles=out_tiles, out_ids=out_ids, out_count=out_count, value_tiles=value_tiles, value_ids=value_ids, value_count=value_count)


EPS = 1e-05

def rms_rows(row_data, gain_row):
    wide = row_data.astype(jnp.float32)
    inverse_rms = lax.rsqrt(lax.optimization_barrier(jnp.mean(wide * wide, axis=-1, keepdims=True)) + EPS)
    return (wide * inverse_rms * gain_row.astype(jnp.float32)).astype(jnp.bfloat16)

def make_grid(tile_data, numbers, filled):
    col_blocks = D // EDGE
    row_blocks = LOCAL // EDGE
    present = jnp.arange(CAP, dtype=jnp.int32)[None, :] < filled[:, None]
    blocks = tile_data.reshape(SHARDS, CAP, EDGE, EDGE)
    blocks = jnp.where(present[:, :, None, None], blocks, jnp.zeros((), blocks.dtype))
    numbers = numbers.reshape(SHARDS, CAP)
    shard_ids = jnp.broadcast_to(jnp.arange(SHARDS, dtype=jnp.int32)[:, None], (SHARDS, CAP))
    grid_data = jnp.zeros((SHARDS, row_blocks, col_blocks, EDGE, EDGE), blocks.dtype)
    grid_data = grid_data.at[shard_ids, numbers // col_blocks, numbers % col_blocks].add(blocks)
    return (grid_data, present, shard_ids, numbers)

def pick_tiles(grid_view, present, shard_ids, numbers):
    col_blocks = D // EDGE
    picked = grid_view[shard_ids, numbers // col_blocks, numbers % col_blocks]
    picked = jnp.where(present[:, :, None, None], picked, jnp.zeros((), picked.dtype))
    return picked.astype(jnp.bfloat16).reshape(SLOTS, EDGE * EDGE)

def one_section(section_inputs):
    layer_input, upstream, query_rows, key_rows, norm_gain, out_tiles, out_ids, out_count, value_tiles, value_ids, value_count = section_inputs
    col_blocks = D // EDGE
    row_blocks = LOCAL // EDGE
    normed = rms_rows(layer_input, norm_gain)
    out_grid, out_present, out_shards, out_numbers = make_grid(out_tiles, out_ids, out_count)
    value_grid, value_present, value_shards, value_numbers = make_grid(value_tiles, value_ids, value_count)
    w_out = out_grid.transpose(0, 1, 3, 2, 4).reshape(D, D)
    w_value = value_grid.transpose(2, 3, 0, 1, 4).reshape(D, D)
    values = jnp.dot(normed, w_value, preferred_element_type=jnp.float32).astype(jnp.bfloat16)
    mixed_grad = jnp.dot(upstream, w_out.T, preferred_element_type=jnp.float32).astype(jnp.bfloat16)
    head_count = D // HEAD

    def split_heads(row_data):
        return row_data.reshape(TOK, head_count, HEAD).transpose(1, 0, 2)
    causal = jnp.arange(TOK)[:, None] >= jnp.arange(TOK)[None, :]

    def per_head(head_item):
        query_head, key_head, value_head, grad_head = head_item
        scores = jnp.dot(query_head, key_head.T, preferred_element_type=jnp.float32) * HEAD ** (-0.5)
        scores = jnp.where(causal, scores, -1e+30)
        row_max = lax.optimization_barrier(jnp.max(scores, axis=-1, keepdims=True))
        weights = jnp.exp(scores - row_max)
        probabilities = (weights / lax.optimization_barrier(jnp.sum(weights, axis=-1, keepdims=True))).astype(jnp.bfloat16)
        attended_head = jnp.dot(probabilities, value_head, preferred_element_type=jnp.float32).astype(jnp.bfloat16)
        value_back = jnp.dot(probabilities.T, grad_head, preferred_element_type=jnp.float32).astype(jnp.bfloat16)
        return (attended_head, value_back)
    attended, value_grads = lax.map(per_head, (split_heads(query_rows), split_heads(key_rows), split_heads(values), split_heads(mixed_grad)))
    attended = attended.transpose(1, 0, 2).reshape(TOK, D)
    value_grads = value_grads.transpose(1, 0, 2).reshape(TOK, D)

    def add_shard(running, shard_pair):
        part_grad, part_weight = shard_pair
        product = jnp.dot(part_grad, part_weight.T, preferred_element_type=jnp.float32)
        return (running + lax.optimization_barrier(product.astype(jnp.bfloat16)).astype(jnp.float32), None)
    shard_grads = value_grads.reshape(TOK, SHARDS, LOCAL).transpose(1, 0, 2)
    shard_weights = w_value.reshape(D, SHARDS, LOCAL).transpose(1, 0, 2)
    summed, _ = lax.scan(add_shard, jnp.zeros((TOK, D), jnp.float32), (shard_grads, shard_weights))
    section_grad = (upstream.astype(jnp.float32) + summed).astype(jnp.bfloat16)
    out_full = jnp.dot(attended.T, upstream, preferred_element_type=jnp.float32)
    out_view = out_full.reshape(SHARDS, row_blocks, EDGE, col_blocks, EDGE).transpose(0, 1, 3, 2, 4)
    out_grad = pick_tiles(out_view, out_present, out_shards, out_numbers)
    value_full = jnp.dot(normed.T, value_grads, preferred_element_type=jnp.float32)
    value_view = value_full.reshape(col_blocks, EDGE, SHARDS, row_blocks, EDGE).transpose(2, 3, 0, 1, 4)
    value_grad = pick_tiles(value_view, value_present, value_shards, value_numbers)
    return (section_grad, out_grad, value_grad)

def reference(layer_input, upstream, query_rows, key_rows, norm_gain, out_tiles, out_ids, out_count, value_tiles, value_ids, value_count):
    section_grad, out_grad, value_grad = lax.map(one_section, (layer_input, upstream, query_rows, key_rows, norm_gain, out_tiles, out_ids, out_count, value_tiles, value_ids, value_count))
    grad_input = jnp.concatenate([section_grad[1:], jnp.zeros_like(section_grad[:1])], axis=0)
    return (grad_input, out_grad, value_grad)
```

```python
import jax
import jax.numpy as jnp
from jax import lax
from jax.experimental import pallas as pl
from jax.experimental.pallas import tpu as pltpu
from jax.sharding import PartitionSpec as P

HEAD = 128
EDGE = 64
EPS = 1e-05
TOK = 256
WIDTH = 256
NZ = 8
NY = 4
CAP = 320
TILES = 512
COLS = 128
MODEL = 8192
HALF = EDGE // 2
CUT_U, CUT_X, CUT_P = 96, 112, 112
EXTRA = 16
BLOCKS = NZ * NY

BF = jnp.bfloat16
F32 = jnp.float32
NN = (((1,), (0,)), ((), ()))
NT = (((1,), (1,)), ((), ()))
TN = (((0,), (0,)), ((), ()))


def dot(a, b, dims=NN):
    return lax.dot_general(a, b, dims, preferred_element_type=F32)


class Links:
    def __init__(self, recv_sems):
        self.recv_sems = recv_sems
        self.used = 0
        place = lax.axis_index("tensor")
        self.place = place
        self.z, self.y = place // NY, place % NY
        self.to = {
            ("z", 1): self.at(1, 0),
            ("z", -1): self.at(-1, 0),
            ("y", 1): self.at(0, 1),
            ("y", -1): self.at(0, -1),
        }

    def at(self, dz, dy):
        return (self.z + (dz + NZ)) % NZ * NY + (self.y + (dy + NY)) % NY

    def semaphore(self):
        self.used += 1
        return self.recv_sems.at[self.used - 1]

    def send(self, src, dst, axis, way, send_sem, recv_sem):
        pltpu.make_async_remote_copy(
            src_ref=src,
            dst_ref=dst,
            send_sem=send_sem,
            recv_sem=recv_sem,
            device_id={"tensor": self.to[(axis, way)]},
            device_id_type=pl.DeviceIdType.MESH,
        ).start()


def wait_for(view, semaphore):
    pltpu.make_async_copy(view, view, semaphore).wait()


WAYS = (1, -1)


class Routes:
    def __init__(self, links, ref, rows, cut, send_sem):
        self.links, self.ref, self.send_sem = links, ref, send_sem
        self.a = (0, cut)
        first = cut // 32 * 16
        self.a_half = {1: (0, first), -1: (first, cut - first)}
        rest = rows - cut
        first = rest // 32 * 16
        self.b = (cut, rest)
        self.b_half = {1: (cut, first), -1: (cut + first, rest - first)}
        self.coming = {}

    def pair(self, key, axis, block, rows, halves, into=None):
        semaphore = self.links.semaphore()
        for way in WAYS:
            part = halves[way] if halves else rows
            src = self.ref.at[block(way), pl.ds(*part)]
            dst = src if into is None else into(way, part[1])
            self.links.send(src, dst, axis, way, self.send_sem, semaphore)
        if halves:
            view = self.ref.at[0, pl.ds(0, rows[1])]
        else:
            view = self.ref.at[pl.ds(0, 2), pl.ds(0, rows[1])]
        self.coming[key] = (view, semaphore)

    def wait(self, *key):
        wait_for(*self.coming.pop(key))

    def sent(self):
        wait_for(self.ref.at[pl.ds(0, BLOCKS - 1)], self.send_sem)


class Gather(Routes):
    def ay(self, step):
        at = self.links.at
        if step > 1:
            self.wait("ay", 1)
        self.pair(
            ("ay", step),
            "y",
            lambda way: at(0, -way * (step - 1)),
            self.a,
            self.a_half if step == 2 else None,
        )

    def az(self, step, *offsets):
        at = self.links.at
        for dy in offsets:
            if step > 1:
                self.wait("az", dy, step - 1)
            elif dy == 2:
                self.wait("ay", 2)
            self.pair(
                ("az", dy, step),
                "z",
                lambda way: at(-way * (step - 1), dy),
                self.a,
                self.a_half if step == 4 else None,
            )

    def bz(self, step):
        at = self.links.at
        if step > 1:
            self.wait("bz", step - 1)
        self.pair(
            ("bz", step),
            "z",
            lambda way: at(-way * (step - 1), 0),
            self.b,
            self.b_half if step == 4 else None,
        )

    def by1(self, *offsets):
        at = self.links.at
        for dz in offsets:
            if dz == 4:
                self.wait("bz", 4)
            self.pair(("by", dz, 1), "y", lambda way: at(dz, 0), self.b, None)

    def by2(self, *offsets):
        at = self.links.at
        for dz in offsets:
            self.wait("by", dz, 1)
            self.pair(("by", dz, 2), "y", lambda way: at(dz, -way), self.b, self.b_half)

    def begin(self):
        self.ay(1)
        self.bz(1)
        self.az(1, 0)
        self.by1(0)

    def steps(self):
        return [
            lambda: (self.ay(2), self.az(1, 1, -1)),
            lambda: (self.bz(2), self.by1(-1, 1)),
            lambda: self.az(2, 0),
            lambda: self.by2(0),
            lambda: self.az(1, 2),
            lambda: self.az(2, 1, -1),
            lambda: (self.bz(3), self.by1(-2, 2)),
            lambda: self.az(3, 0),
            lambda: self.by2(-1, 1),
            lambda: self.az(2, 2),
            lambda: self.az(3, 1, -1),
            lambda: (self.bz(4), self.by1(-3, 3)),
            lambda: self.az(4, 0),
            lambda: self.by2(-2, 2),
            lambda: self.az(3, 2),
            lambda: self.az(4, 1, -1),
            lambda: self.by1(4),
            lambda: self.by2(-3, 3),
            lambda: self.az(4, 2),
            lambda: self.by2(4),
            lambda: self.finish(),
        ]

    def finish(self):
        for key in sorted(self.coming):
            self.wait(*key)


class Scatter(Routes):
    def __init__(self, links, ref, cut, send_sem, az_in, by_in, ay_in, bz_in):
        super().__init__(links, ref, TOK, cut, send_sem)
        self.az_in, self.by_in, self.ay_in, self.bz_in = az_in, by_in, ay_in, bz_in

    def add(self, block, rows, *got):
        part = self.ref[block, pl.ds(*rows)].astype(F32)
        for more in got:
            part = part + more.astype(F32)
        self.ref[block, pl.ds(*rows)] = part.astype(BF)

    def az(self, step, *offsets):
        at = self.links.at
        for dy in offsets:
            if step > 1:
                self.wait("az", dy, step - 1)
                for way in WAYS:
                    rows = self.a if step > 2 else self.a_half[way]
                    got = self.az_in[(way + 1) // 2, step - 2, dy + 1, pl.ds(0, rows[1])]
                    self.add(at(way * (5 - step), dy), rows, got)
            self.pair(
                ("az", dy, step),
                "z",
                lambda way: at(way * (5 - step), dy),
                self.a,
                self.a_half if step == 1 else None,
                lambda way, size: self.az_in.at[(way + 1) // 2, step - 1, dy + 1, pl.ds(0, size)],
            )

    def az_done(self, *offsets):
        for dy in offsets:
            self.wait("az", dy, 4)
            self.add(self.links.at(0, dy), self.a, self.az_in[0, 3, dy + 1], self.az_in[1, 3, dy + 1])

    def by(self, step, *offsets):
        at = self.links.at
        for dz in offsets:
            if step > 1:
                self.wait("by", dz, 1)
                for way in WAYS:
                    rows = self.b_half[way]
                    got = self.by_in[(way + 1) // 2, 0, dz + 3, pl.ds(0, rows[1])]
                    self.add(at(dz, way), rows, got)
            self.pair(
                ("by", dz, step),
                "y",
                lambda way: at(dz, way * (3 - step)),
                self.b,
                self.b_half if step == 1 else None,
                lambda way, size: self.by_in.at[(way + 1) // 2, step - 1, dz + 3, pl.ds(0, size)],
            )

    def by_done(self, *offsets):
        for dz in offsets:
            self.wait("by", dz, 2)
            self.add(self.links.at(dz, 0), self.b, self.by_in[0, 1, dz + 3], self.by_in[1, 1, dz + 3])

    def ay(self, step):
        at = self.links.at
        if step > 1:
            self.wait("ay", 1)
            for way in WAYS:
                rows = self.a_half[way]
                self.add(at(0, way), rows, self.ay_in[(way + 1) // 2, 0, pl.ds(0, rows[1])])
        self.pair(
            ("ay", step),
            "y",
            lambda way: at(0, way * (3 - step)),
            self.a,
            self.a_half if step == 1 else None,
            lambda way, size: self.ay_in.at[(way + 1) // 2, step - 1, pl.ds(0, size)],
        )

    def bz(self, step):
        at = self.links.at
        if step > 1:
            self.wait("bz", step - 1)
            for way in WAYS:
                rows = self.b if step > 2 else self.b_half[way]
                got = self.bz_in[(way + 1) // 2, step - 2, pl.ds(0, rows[1])]
                self.add(at(way * (5 - step), 0), rows, got)
        self.pair(
            ("bz", step),
            "z",
            lambda way: at(way * (5 - step), 0),
            self.b,
            self.b_half if step == 1 else None,
            lambda way, size: self.bz_in.at[(way + 1) // 2, step - 1, pl.ds(0, size)],
        )

    def begin(self):
        self.az(1, 2)
        self.by(1, 4)
        self.az(1, 1, -1)
        self.by(1, -3, 3)
        self.az(1, 0)
        self.by(1, -2, 2)

    def steps(self):
        return [
            lambda: self.az(2, 2),
            lambda: self.by(2, 4),
            lambda: self.az(2, 1, -1),
            lambda: (self.by(2, -3, 3), self.by(1, -1, 1)),
            lambda: self.az(2, 0),
            lambda: self.az(3, 2),
            lambda: (self.by_done(4), self.bz(1)),
            lambda: (self.by(2, -2, 2), self.by(1, 0)),
            lambda: self.az(3, 1, -1),
            lambda: (self.by_done(-3, 3), self.bz(2)),
            lambda: self.az(3, 0),
            lambda: self.az(4, 2),
            lambda: self.by(2, -1, 1),
            lambda: (self.by_done(-2, 2), self.bz(3)),
            lambda: self.az(4, 1, -1),
            lambda: self.by(2, 0),
            lambda: (self.az_done(2), self.ay(1)),
            lambda: (self.by_done(-1, 1), self.bz(4)),
            lambda: self.az(4, 0),
            lambda: (self.az_done(1, -1), self.ay(2)),
            lambda: self.by_done(0),
            lambda: self.az_done(0),
        ]

    def upper(self):
        self.wait("ay", 2)
        total = self.ref[self.links.place, pl.ds(*self.a)].astype(F32)
        return total + self.ay_in[0, 1].astype(F32) + self.ay_in[1, 1].astype(F32)

    def lower(self):
        self.wait("bz", 4)
        total = self.ref[self.links.place, pl.ds(*self.b)].astype(F32)
        return total + self.bz_in[0, 3].astype(F32) + self.bz_in[1, 3].astype(F32)


def blended(steps, more, start=0.0, end=1.0):
    out, done = [], 0
    for i, step in enumerate(steps):
        reached = (i / len(steps) - start) / (end - start)
        upto = min(len(more), max(0, int(len(more) * reached)))
        out += more[done:upto]
        done = max(done, upto)
        out.append(step)
    return out + more[done:]


def kernel(
    out_ids, val_ids, out_count, val_count, gain, x_hbm, u_hbm, q_hbm, k_hbm, out_hbm, val_hbm,
    grad_input, out_grad, value_grad,
    gu, gx, xin, qin, kin, t_out, t_val, place_out, pick_out, place_val, pick_val, dense, w_out, w_val, probs, part,
    acc, wide_grads, vals, grads, scaled, att_t, az_in, by_in, ay_in, bz_in, final, passed,
    load_sems, send_sems, recv_sems,
):
    links = Links(recv_sems)
    place = links.place
    section = lax.axis_index("section")
    sections = lax.axis_size("section")
    before, after = (section + sections - 1) % sections, (section + 1) % sections

    loads = [
        pltpu.make_async_copy(src, dst, load_sems.at[i])
        for i, (src, dst) in enumerate(
            (
                (u_hbm.at[0], gu.at[place]),
                (x_hbm.at[0], xin),
                (out_hbm.at[0], t_out),
                (val_hbm.at[0], t_val),
                (q_hbm.at[0], qin),
                (k_hbm.at[0], kin),
            )
        )
    ]
    for load in loads:
        load.start()

    barrier = pltpu.get_barrier_semaphore()
    for to in links.to.values():
        pl.semaphore_signal(
            barrier, inc=1, device_id={"tensor": to}, device_id_type=pl.DeviceIdType.MESH
        )
    for to in (before, after):
        pl.semaphore_signal(
            barrier, inc=1, device_id={"section": to}, device_id_type=pl.DeviceIdType.MESH
        )

    gather_u = Gather(links, gu, TOK, CUT_U, send_sems.at[0])
    gather_x = Gather(links, gx, TOK + EXTRA, CUT_X, send_sems.at[1])
    scatter = Scatter(links, part, CUT_P, send_sems.at[2], az_in, by_in, ay_in, bz_in)

    lane = lax.broadcasted_iota(jnp.int32, (HALF, HEAD), 1)
    left = lane < EDGE
    rows_at = lax.broadcasted_iota(jnp.int32, (WIDTH, WIDTH), 0)
    cols_at = lax.broadcasted_iota(jnp.int32, (WIDTH, WIDTH), 1)
    inner = cols_at % EDGE
    natural = cols_at - inner + 2 * (inner % HALF) + inner // HALF
    order = (rows_at == natural).astype(F32).astype(BF)
    same = rows_at == cols_at

    def pair_out(first, second):
        evens = jnp.where(left, first, pltpu.roll(second, EDGE, 1))
        odds = jnp.where(left, pltpu.roll(first, EDGE, 1), second)
        return evens, odds

    def prepare_x():
        loads[1].wait()
        x = xin[...].astype(F32)
        row = pl.multiple_of(place * WIDTH, WIDTH)
        scaled_x = (x * gain[0:1, pl.ds(row, WIDTH)].astype(F32)).astype(BF)
        gx[place, pl.ds(0, TOK)] = dot(scaled_x, order).astype(BF)
        squares = jnp.sum(x * x, axis=1, keepdims=True)
        flat = jnp.sum(jnp.where(same, squares, 0.0), axis=0, keepdims=True)
        high = flat.astype(BF).astype(F32)
        middle = (flat - high).astype(BF).astype(F32)
        low = flat - high - middle
        at_row = lax.broadcasted_iota(jnp.int32, (EXTRA, TOK), 0)
        ride = jnp.where(at_row == 0, high, jnp.where(at_row == 1, middle, jnp.where(at_row == 2, low, 0.0)))
        gx[place, pl.ds(TOK, EXTRA)] = ride.astype(BF)

    def placers(ids, count, placer, picker):
        position = lax.broadcasted_iota(jnp.int32, (TILES, CAP), 0)
        slot = lax.broadcasted_iota(jnp.int32, (TILES, CAP), 1)
        held = (position == ids[...]) & (slot < count[...])
        placer[...] = held.astype(F32).astype(BF)
        across = lax.broadcasted_iota(jnp.int32, (CAP, CAP), 0) == lax.broadcasted_iota(jnp.int32, (CAP, CAP), 1)
        picker[...] = dot(across.astype(F32).astype(BF), placer[...], NT).astype(BF)

    def spread(tiles, placer, first, last):
        @pl.loop(first, last)
        def _(k):
            cols = pl.ds(pl.multiple_of(k * 256, 256), 256)
            for upper in range(0, TILES, 256):
                placed = dot(placer[pl.ds(upper, 256), :], tiles[:, cols])
                for row in range(0, 256, 8):
                    for side in range(2):
                        at = (upper + row) * 32 + 2 * k + side
                        dense[pl.ds(at, 8, stride=32), :] = placed[row : row + 8, side * HEAD : (side + 1) * HEAD]

    def gather_back(tiles, picker, first, last):
        @pl.loop(first, last)
        def _(k):
            cols = pl.ds(pl.multiple_of(k * 256, 256), 256)
            sides = [
                jnp.concatenate(
                    [dense[pl.ds(row * 32 + 2 * k + side, 8, stride=32), :] for row in range(0, TILES, 8)], axis=0
                ).astype(BF)
                for side in range(2)
            ]
            tiles[:, cols] = dot(picker[...], jnp.concatenate(sides, axis=1)).astype(BF)

    def tile(at):
        return dense[pl.ds(pl.multiple_of(at * 32, 32), 32), :]

    def build_out(first, last):
        @pl.loop(first, last)
        def _(g):
            for r in range(4):
                for pair in range(2):
                    at = r * COLS + g * 4 + 2 * pair
                    evens, odds = pair_out(tile(at), tile(at + 1))
                    cols = pl.ds(pair * HEAD, HEAD)
                    w_out[g, pl.ds(r * EDGE, HALF), cols] = evens.astype(BF)
                    w_out[g, pl.ds(r * EDGE + HALF, HALF), cols] = odds.astype(BF)

    def build_val(first, last):
        @pl.loop(first, last)
        def _(g):
            for c in range(4):
                for pair in range(2):
                    at = 2 * pair * COLS + g * 4 + c
                    evens, odds = pair_out(tile(at), tile(at + COLS))
                    cols = pl.ds(pair * HEAD, HEAD)
                    w_val[g, pl.ds(c * EDGE, HALF), cols] = evens.astype(BF)
                    w_val[g, pl.ds(c * EDGE + HALF, HALF), cols] = odds.astype(BF)

    def attention(head):
        cols = pl.ds(head * HEAD, HEAD)
        scores = dot(qin[:, cols], kin[:, cols], NT) * HEAD ** (-0.5)
        scores = jnp.where(rows_at >= cols_at, scores, -1e30)
        weights = jnp.exp(scores - jnp.max(scores, axis=1, keepdims=True))
        probs[head] = (weights / jnp.sum(weights, axis=1, keepdims=True)).astype(BF)

    def mixed(first, last):
        total = None
        for g in range(first, last):
            term = dot(gu[g], w_out[g], NT)
            total = term if total is None else total + term
        acc[...] = total if first == 0 else acc[...] + total

    def value_grads():
        mixed_grad = dot(acc[...].astype(BF), order, NT).astype(BF)
        for head in range(2):
            cols = pl.ds(head * HEAD, HEAD)
            back = dot(probs[head], mixed_grad[:, head * HEAD : (head + 1) * HEAD], TN)
            wide_grads[:, cols] = back
            grads[:, cols] = back.astype(BF)

    def partial_terms(first, last):
        for g in range(first, last):
            part[g] = dot(grads[...], w_val[g], NT).astype(BF)

    def values(first, last):
        total = None
        for g in range(first, last):
            term = dot(gx[g, pl.ds(0, TOK)], w_val[g])
            total = term if total is None else total + term
        acc[...] = total if first == 0 else acc[...] + total

    def attended():
        ride = jnp.zeros((EXTRA, TOK), F32)
        for g in range(BLOCKS):
            ride = ride + gx[g, pl.ds(TOK, EXTRA)].astype(F32)
        flat = jnp.sum(ride, axis=0, keepdims=True)
        squares = jnp.sum(jnp.where(same, flat, 0.0), axis=1, keepdims=True)
        inverse = lax.rsqrt(squares / MODEL + EPS)
        vals[...] = (acc[...] * inverse).astype(BF)
        scaled[...] = (wide_grads[...] * inverse).astype(BF)
        for head in range(2):
            cols = pl.ds(head * HEAD, HEAD)
            grads[:, cols] = dot(probs[head], vals[:, cols]).astype(BF)
        att_t[...] = dot(order, grads[...], (((0,), (1,)), ((), ()))).astype(BF)

    def put(at, value):
        dense[pl.ds(pl.multiple_of(at * 32, 32), 32), :] = value

    def full_out(first, last):
        @pl.loop(first, last)
        def _(g):
            block = dot(att_t[...], gu[g])
            for r in range(4):
                for pair in range(2):
                    cols = slice(pair * HEAD, (pair + 1) * HEAD)
                    evens = block[r * EDGE : r * EDGE + HALF, cols]
                    odds = block[r * EDGE + HALF : (r + 1) * EDGE, cols]
                    one, two = pair_out(evens, odds)
                    at = r * COLS + g * 4 + 2 * pair
                    put(at, one)
                    put(at + 1, two)

    def full_val(first, last):
        @pl.loop(first, last)
        def _(g):
            block = dot(gx[g, pl.ds(0, TOK)], scaled[...], TN)
            for c in range(4):
                for pair in range(2):
                    cols = slice(pair * HEAD, (pair + 1) * HEAD)
                    evens = block[c * EDGE : c * EDGE + HALF, cols]
                    odds = block[c * EDGE + HALF : (c + 1) * EDGE, cols]
                    one, two = pair_out(evens, odds)
                    at = 2 * pair * COLS + g * 4 + c
                    put(at, one)
                    put(at + COLS, two)

    def cut(function, parts, total, *given):
        size = total // parts
        return [lambda i=i: function(*given, i * size, (i + 1) * size) for i in range(parts)]

    stores = [
        pltpu.make_async_copy(t_out, out_grad.at[0], load_sems.at[6]),
        pltpu.make_async_copy(t_val, value_grad.at[0], load_sems.at[7]),
    ]

    alone = [
        lambda: placers(out_ids, out_count, place_out, pick_out),
        lambda: placers(val_ids, val_count, place_val, pick_val),
        loads[2].wait,
        *cut(spread, 8, 16, t_out, place_out),
        *cut(build_out, 8, BLOCKS),
        loads[3].wait,
        *cut(spread, 8, 16, t_val, place_val),
        *cut(build_val, 8, BLOCKS),
        loads[4].wait,
        loads[5].wait,
        lambda: attention(0),
        lambda: attention(1),
    ]
    back = [*cut(mixed, 8, BLOCKS), value_grads, *cut(partial_terms, 8, BLOCKS), scatter.begin]
    beside = [
        *cut(values, 8, BLOCKS),
        attended,
        *cut(full_out, 8, BLOCKS),
        *cut(gather_back, 8, 16, t_out, pick_out),
        stores[0].start,
        *cut(full_val, 8, BLOCKS),
        *cut(gather_back, 8, 16, t_val, pick_val),
        stores[1].start,
    ]

    loads[0].wait()
    pl.semaphore_wait(barrier, 6)
    gather_u.begin()
    prepare_x()

    steps_x = [gather_x.begin, *gather_x.steps()]
    early, middle = X_CUTS
    plan = blended(blended(gather_u.steps(), steps_x[:early], X_START), alone, 0.0, 1.0)
    plan += blended(back, steps_x[early:middle])
    sums = scatter.steps()
    plan += blended(sums[:SUMS_FIRST], steps_x[middle:])
    plan += blended(sums[SUMS_FIRST:], beside)
    for step in plan:
        step()

    def finish(rows, total):
        high = total.astype(BF)
        low = (total - high.astype(F32)).astype(BF)
        summed = dot(high, order, NT) + dot(low, order, NT)
        final[pl.ds(*rows)] = (gu[place, pl.ds(*rows)].astype(F32) + summed).astype(BF)

    finish(scatter.b, scatter.lower())
    finish(scatter.a, scatter.upper())

    hand_on = pltpu.make_async_remote_copy(
        src_ref=final,
        dst_ref=passed,
        send_sem=load_sems.at[9],
        recv_sem=load_sems.at[10],
        device_id={"section": before},
        device_id_type=pl.DeviceIdType.MESH,
    )

    @pl.when(section > 0)
    def _():
        hand_on.start()

    @pl.when(section == sections - 1)
    def _():
        passed[...] = jnp.zeros_like(passed)

    for routes in (gather_u, gather_x, scatter):
        routes.sent()

    @pl.when(section < sections - 1)
    def _():
        hand_on.wait_recv()

    last = pltpu.make_async_copy(passed, grad_input.at[0], load_sems.at[8])
    last.start()

    @pl.when(section > 0)
    def _():
        hand_on.wait_send()

    for store in stores:
        store.wait()
    last.wait()


X_CUTS = (9, 16)
X_START = 0.25
SUMS_FIRST = 6
PAIRS = 3 * 38


def backward(x, u, q, k, gain, out_tiles, out_ids, out_count, val_tiles, val_ids, val_count):
    vmem = pl.BlockSpec(memory_space=pltpu.VMEM)
    hbm = pl.BlockSpec(memory_space=pl.ANY)
    rest = TOK - CUT_P
    return pl.pallas_call(
        kernel,
        out_shape=(
            jax.ShapeDtypeStruct((1, TOK, WIDTH), BF),
            jax.ShapeDtypeStruct((1, CAP, EDGE * EDGE), BF),
            jax.ShapeDtypeStruct((1, CAP, EDGE * EDGE), BF),
        ),
        in_specs=[vmem] * 5 + [hbm] * 6,
        out_specs=(hbm, hbm, hbm),
        scratch_shapes=[
            pltpu.VMEM((BLOCKS, TOK, WIDTH), BF),
            pltpu.VMEM((BLOCKS, TOK + EXTRA, WIDTH), BF),
            pltpu.VMEM((TOK, WIDTH), BF),
            pltpu.VMEM((TOK, WIDTH), BF),
            pltpu.VMEM((TOK, WIDTH), BF),
            pltpu.VMEM((CAP, EDGE * EDGE), BF),
            pltpu.VMEM((CAP, EDGE * EDGE), BF),
            pltpu.VMEM((TILES, CAP), BF),
            pltpu.VMEM((CAP, TILES), BF),
            pltpu.VMEM((TILES, CAP), BF),
            pltpu.VMEM((CAP, TILES), BF),
            pltpu.VMEM((TILES * 32, HEAD), F32),
            pltpu.VMEM((BLOCKS, WIDTH, WIDTH), BF),
            pltpu.VMEM((BLOCKS, WIDTH, WIDTH), BF),
            pltpu.VMEM((2, TOK, TOK), BF),
            pltpu.VMEM((BLOCKS, TOK, WIDTH), BF),
            pltpu.VMEM((TOK, WIDTH), F32),
            pltpu.VMEM((TOK, WIDTH), F32),
            pltpu.VMEM((TOK, WIDTH), BF),
            pltpu.VMEM((TOK, WIDTH), BF),
            pltpu.VMEM((TOK, WIDTH), BF),
            pltpu.VMEM((WIDTH, TOK), BF),
            pltpu.VMEM((2, 4, NY, CUT_P, WIDTH), BF),
            pltpu.VMEM((2, 2, NZ, rest, WIDTH), BF),
            pltpu.VMEM((2, 2, CUT_P, WIDTH), BF),
            pltpu.VMEM((2, 4, rest, WIDTH), BF),
            pltpu.VMEM((TOK, WIDTH), BF),
            pltpu.VMEM((TOK, WIDTH), BF),
            pltpu.SemaphoreType.DMA((11,)),
            pltpu.SemaphoreType.DMA((3,)),
            pltpu.SemaphoreType.DMA((PAIRS,)),
        ],
        compiler_params=pltpu.CompilerParams(
            collective_id=0, has_side_effects=True, vmem_limit_bytes=46 * 1024 * 1024
        ),
        cost_estimate=pl.CostEstimate(flops=12 * 2**30, bytes_accessed=12 * 2**20, transcendentals=2**17),
    )(out_ids, val_ids, out_count, val_count, gain, x, u, q, k, out_tiles, val_tiles)


def per_device(
    layer_input, upstream, query_rows, key_rows, norm_gain, out_tiles, out_ids, out_count, value_tiles, value_ids,
    value_count,
):
    return backward(
        layer_input,
        upstream,
        query_rows,
        key_rows,
        norm_gain,
        out_tiles,
        out_ids,
        out_count,
        value_tiles,
        value_ids,
        value_count,
    )


def solution(mesh):
    rows = P("section", None, "tensor")
    tiles = P("section", "tensor", None)
    pair = P("section", "tensor")
    return jax.shard_map(
        per_device,
        mesh=mesh,
        in_specs=(rows, rows, rows, rows, P("section", None), tiles, pair, pair, tiles, pair, pair),
        out_specs=(rows, tiles, tiles),
        check_vma=False,
    )
```

```python
import jax
import jax.numpy as jnp
from jax import lax
from jax.experimental import pallas as pl
from jax.experimental.pallas import tpu as pltpu
from jax.sharding import PartitionSpec as P

HEAD = 128
EDGE = 64
EPS = 1e-05
TOK = 256
WIDTH = 256
NZ = 8
NY = 4
CAP = 320
TILES = 512
COLS = 128
MODEL = 8192
HALF = EDGE // 2
CUT_U, CUT_X, CUT_P = 96, 112, 112
EXTRA = 16
BLOCKS = NZ * NY
PITCH = 33

BF = jnp.bfloat16
F32 = jnp.float32
NN = (((1,), (0,)), ((), ()))
NT = (((1,), (1,)), ((), ()))
TN = (((0,), (0,)), ((), ()))


def dot(a, b, dims=NN):
    return lax.dot_general(a, b, dims, preferred_element_type=F32)


class Links:
    def __init__(self, recv_sems):
        self.recv_sems = recv_sems
        self.used = 0
        place = lax.axis_index("tensor")
        self.place = place
        self.z, self.y = place // NY, place % NY
        self.to = {
            ("z", 1): self.at(1, 0),
            ("z", -1): self.at(-1, 0),
            ("y", 1): self.at(0, 1),
            ("y", -1): self.at(0, -1),
        }

    def at(self, dz, dy):
        return (self.z + (dz + NZ)) % NZ * NY + (self.y + (dy + NY)) % NY

    def semaphore(self):
        self.used += 1
        return self.recv_sems.at[self.used - 1]

    def send(self, src, dst, axis, way, send_sem, recv_sem):
        pltpu.make_async_remote_copy(
            src_ref=src,
            dst_ref=dst,
            send_sem=send_sem,
            recv_sem=recv_sem,
            device_id={"tensor": self.to[(axis, way)]},
            device_id_type=pl.DeviceIdType.MESH,
        ).start()


def wait_for(view, semaphore):
    pltpu.make_async_copy(view, view, semaphore).wait()


WAYS = (1, -1)


class Routes:
    def __init__(self, links, ref, rows, cut, send_sem):
        self.links, self.ref, self.send_sem = links, ref, send_sem
        self.a = (0, cut)
        first = cut // 32 * 16
        self.a_half = {1: (0, first), -1: (first, cut - first)}
        rest = rows - cut
        first = rest // 32 * 16
        self.b = (cut, rest)
        self.b_half = {1: (cut, first), -1: (cut + first, rest - first)}
        self.coming = {}

    def pair(self, key, axis, block, rows, halves, into=None):
        semaphore = self.links.semaphore()
        for way in WAYS:
            part = halves[way] if halves else rows
            src = self.ref.at[block(way), pl.ds(*part)]
            dst = src if into is None else into(way, part[1])
            self.links.send(src, dst, axis, way, self.send_sem, semaphore)
        if halves:
            view = self.ref.at[0, pl.ds(0, rows[1])]
        else:
            view = self.ref.at[pl.ds(0, 2), pl.ds(0, rows[1])]
        self.coming[key] = (view, semaphore)

    def wait(self, *key):
        wait_for(*self.coming.pop(key))

    def sent(self):
        wait_for(self.ref.at[pl.ds(0, BLOCKS - 1)], self.send_sem)


class Gather(Routes):
    def ay(self, step):
        at = self.links.at
        if step > 1:
            self.wait("ay", 1)
        self.pair(
            ("ay", step),
            "y",
            lambda way: at(0, -way * (step - 1)),
            self.a,
            self.a_half if step == 2 else None,
        )

    def az(self, step, *offsets):
        at = self.links.at
        for dy in offsets:
            if step > 1:
                self.wait("az", dy, step - 1)
            elif dy == 2:
                self.wait("ay", 2)
            self.pair(
                ("az", dy, step),
                "z",
                lambda way: at(-way * (step - 1), dy),
                self.a,
                self.a_half if step == 4 else None,
            )

    def bz(self, step):
        at = self.links.at
        if step > 1:
            self.wait("bz", step - 1)
        self.pair(
            ("bz", step),
            "z",
            lambda way: at(-way * (step - 1), 0),
            self.b,
            self.b_half if step == 4 else None,
        )

    def by1(self, *offsets):
        at = self.links.at
        for dz in offsets:
            if dz == 4:
                self.wait("bz", 4)
            self.pair(("by", dz, 1), "y", lambda way: at(dz, 0), self.b, None)

    def by2(self, *offsets):
        at = self.links.at
        for dz in offsets:
            self.wait("by", dz, 1)
            self.pair(("by", dz, 2), "y", lambda way: at(dz, -way), self.b, self.b_half)

    def begin(self):
        self.ay(1)
        self.bz(1)
        self.az(1, 0)
        self.by1(0)

    def steps(self):
        return [
            lambda: (self.ay(2), self.az(1, 1, -1)),
            lambda: (self.bz(2), self.by1(-1, 1)),
            lambda: self.az(2, 0),
            lambda: self.by2(0),
            lambda: self.az(1, 2),
            lambda: self.az(2, 1, -1),
            lambda: (self.bz(3), self.by1(-2, 2)),
            lambda: self.az(3, 0),
            lambda: self.by2(-1, 1),
            lambda: self.az(2, 2),
            lambda: self.az(3, 1, -1),
            lambda: (self.bz(4), self.by1(-3, 3)),
            lambda: self.az(4, 0),
            lambda: self.by2(-2, 2),
            lambda: self.az(3, 2),
            lambda: self.az(4, 1, -1),
            lambda: self.by1(4),
            lambda: self.by2(-3, 3),
            lambda: self.az(4, 2),
            lambda: self.by2(4),
            lambda: self.finish(),
        ]

    def finish(self):
        for key in sorted(self.coming):
            self.wait(*key)


class Scatter(Routes):
    def __init__(self, links, ref, cut, send_sem, az_in, by_in, ay_in, bz_in):
        super().__init__(links, ref, TOK, cut, send_sem)
        self.az_in, self.by_in, self.ay_in, self.bz_in = az_in, by_in, ay_in, bz_in

    def add(self, block, rows, *got):
        part = self.ref[block, pl.ds(*rows)].astype(F32)
        for more in got:
            part = part + more.astype(F32)
        self.ref[block, pl.ds(*rows)] = part.astype(BF)

    def az(self, step, *offsets):
        at = self.links.at
        for dy in offsets:
            if step > 1:
                self.wait("az", dy, step - 1)
                for way in WAYS:
                    rows = self.a if step > 2 else self.a_half[way]
                    got = self.az_in[(way + 1) // 2, step - 2, dy + 1, pl.ds(0, rows[1])]
                    self.add(at(way * (5 - step), dy), rows, got)
            self.pair(
                ("az", dy, step),
                "z",
                lambda way: at(way * (5 - step), dy),
                self.a,
                self.a_half if step == 1 else None,
                lambda way, size: self.az_in.at[(way + 1) // 2, step - 1, dy + 1, pl.ds(0, size)],
            )

    def az_done(self, *offsets):
        for dy in offsets:
            self.wait("az", dy, 4)
            self.add(self.links.at(0, dy), self.a, self.az_in[0, 3, dy + 1], self.az_in[1, 3, dy + 1])

    def by(self, step, *offsets):
        at = self.links.at
        for dz in offsets:
            if step > 1:
                self.wait("by", dz, 1)
                for way in WAYS:
                    rows = self.b_half[way]
                    got = self.by_in[(way + 1) // 2, 0, dz + 3, pl.ds(0, rows[1])]
                    self.add(at(dz, way), rows, got)
            self.pair(
                ("by", dz, step),
                "y",
                lambda way: at(dz, way * (3 - step)),
                self.b,
                self.b_half if step == 1 else None,
                lambda way, size: self.by_in.at[(way + 1) // 2, step - 1, dz + 3, pl.ds(0, size)],
            )

    def by_done(self, *offsets):
        for dz in offsets:
            self.wait("by", dz, 2)
            self.add(self.links.at(dz, 0), self.b, self.by_in[0, 1, dz + 3], self.by_in[1, 1, dz + 3])

    def ay(self, step):
        at = self.links.at
        if step > 1:
            self.wait("ay", 1)
            for way in WAYS:
                rows = self.a_half[way]
                self.add(at(0, way), rows, self.ay_in[(way + 1) // 2, 0, pl.ds(0, rows[1])])
        self.pair(
            ("ay", step),
            "y",
            lambda way: at(0, way * (3 - step)),
            self.a,
            self.a_half if step == 1 else None,
            lambda way, size: self.ay_in.at[(way + 1) // 2, step - 1, pl.ds(0, size)],
        )

    def bz(self, step):
        at = self.links.at
        if step > 1:
            self.wait("bz", step - 1)
            for way in WAYS:
                rows = self.b if step > 2 else self.b_half[way]
                got = self.bz_in[(way + 1) // 2, step - 2, pl.ds(0, rows[1])]
                self.add(at(way * (5 - step), 0), rows, got)
        self.pair(
            ("bz", step),
            "z",
            lambda way: at(way * (5 - step), 0),
            self.b,
            self.b_half if step == 1 else None,
            lambda way, size: self.bz_in.at[(way + 1) // 2, step - 1, pl.ds(0, size)],
        )

    def begin(self):
        self.az(1, 2)
        self.by(1, 4)
        self.az(1, 1, -1)
        self.by(1, -3, 3)
        self.az(1, 0)
        self.by(1, -2, 2)

    def steps(self):
        return [
            lambda: self.az(2, 2),
            lambda: self.by(2, 4),
            lambda: self.az(2, 1, -1),
            lambda: (self.by(2, -3, 3), self.by(1, -1, 1)),
            lambda: self.az(2, 0),
            lambda: self.az(3, 2),
            lambda: (self.by_done(4), self.bz(1)),
            lambda: (self.by(2, -2, 2), self.by(1, 0)),
            lambda: self.az(3, 1, -1),
            lambda: (self.by_done(-3, 3), self.bz(2)),
            lambda: self.az(3, 0),
            lambda: self.az(4, 2),
            lambda: self.by(2, -1, 1),
            lambda: (self.by_done(-2, 2), self.bz(3)),
            lambda: self.az(4, 1, -1),
            lambda: self.by(2, 0),
            lambda: (self.az_done(2), self.ay(1)),
            lambda: (self.by_done(-1, 1), self.bz(4)),
            lambda: self.az(4, 0),
            lambda: (self.az_done(1, -1), self.ay(2)),
            lambda: self.by_done(0),
            lambda: self.az_done(0),
        ]

    def upper(self):
        self.wait("ay", 2)
        total = self.ref[self.links.place, pl.ds(*self.a)].astype(F32)
        return total + self.ay_in[0, 1].astype(F32) + self.ay_in[1, 1].astype(F32)

    def lower(self):
        self.wait("bz", 4)
        total = self.ref[self.links.place, pl.ds(*self.b)].astype(F32)
        return total + self.bz_in[0, 3].astype(F32) + self.bz_in[1, 3].astype(F32)


def blended(steps, more, start=0.0, end=1.0):
    out, done = [], 0
    for i, step in enumerate(steps):
        reached = (i / len(steps) - start) / (end - start)
        upto = min(len(more), max(0, int(len(more) * reached)))
        out += more[done:upto]
        done = max(done, upto)
        out.append(step)
    return out + more[done:]


def kernel(
    out_ids_hbm, val_ids_hbm, out_count_hbm, val_count_hbm, gain_hbm, x_hbm, u_hbm, q_hbm, k_hbm, out_hbm, val_hbm,
    grad_input, out_grad, value_grad,
    out_ids, val_ids, out_count, val_count, gain, gu, gx, xin, qin, kin, t_out, t_val, place_out, pick_out, place_val, pick_val, dense, w_out, w_val, probs, probs_t,
    acc, wide_grads, vals, grads, scaled, att_t, az_in, by_in, ay_in, bz_in, final, passed,
    load_sems, send_sems, recv_sems,
):
    links = Links(recv_sems)
    part = w_out
    place = links.place
    section = lax.axis_index("section")
    sections = lax.axis_size("section")
    before, after = (section + sections - 1) % sections, (section + 1) % sections

    loads = [
        pltpu.make_async_copy(src, dst, load_sems.at[i])
        for i, (src, dst) in enumerate(
            (
                (u_hbm.at[0], gu.at[place]),
                (x_hbm.at[0], xin),
                (out_hbm.at[0], t_out),
                (val_hbm.at[0], t_val),
                (q_hbm.at[0], qin),
                (k_hbm.at[0], kin),
                (gain_hbm, gain),
                (out_ids_hbm, out_ids),
                (val_ids_hbm, val_ids),
                (out_count_hbm, out_count),
                (val_count_hbm, val_count),
            )
        )
    ]
    for load in loads:
        load.start()

    barrier = pltpu.get_barrier_semaphore()
    for to in links.to.values():
        pl.semaphore_signal(
            barrier, inc=1, device_id={"tensor": to}, device_id_type=pl.DeviceIdType.MESH
        )
    for to in (before, after):
        pl.semaphore_signal(
            barrier, inc=1, device_id={"section": to}, device_id_type=pl.DeviceIdType.MESH
        )

    gather_u = Gather(links, gu, TOK, CUT_U, send_sems.at[0])
    gather_x = Gather(links, gx, TOK + EXTRA, CUT_X, send_sems.at[1])
    scatter = Scatter(links, part, CUT_P, send_sems.at[2], az_in, by_in, ay_in, bz_in)

    lane = lax.broadcasted_iota(jnp.int32, (HALF, HEAD), 1)
    left = lane < EDGE
    rows_at = lax.broadcasted_iota(jnp.int32, (WIDTH, WIDTH), 0)
    cols_at = lax.broadcasted_iota(jnp.int32, (WIDTH, WIDTH), 1)
    inner = cols_at % EDGE
    natural = cols_at - inner + 2 * (inner % HALF) + inner // HALF
    order = (rows_at == natural).astype(F32).astype(BF)
    same = rows_at == cols_at

    def pair_out(first, second):
        evens = jnp.where(left, first, pltpu.roll(second, EDGE, 1))
        odds = jnp.where(left, pltpu.roll(first, EDGE, 1), second)
        return evens, odds

    def prepare_x():
        loads[1].wait()
        loads[6].wait()
        x = xin[...].astype(F32)
        row = pl.multiple_of(place * WIDTH, WIDTH)
        scaled_x = (x * gain[0:1, pl.ds(row, WIDTH)].astype(F32)).astype(BF)
        gx[place, pl.ds(0, TOK)] = dot(scaled_x, order).astype(BF)
        squares = jnp.sum(x * x, axis=1, keepdims=True)
        flat = jnp.sum(jnp.where(same, squares, 0.0), axis=0, keepdims=True)
        high = flat.astype(BF).astype(F32)
        middle = (flat - high).astype(BF).astype(F32)
        low = flat - high - middle
        at_row = lax.broadcasted_iota(jnp.int32, (EXTRA, TOK), 0)
        ride = jnp.where(at_row == 0, high, jnp.where(at_row == 1, middle, jnp.where(at_row == 2, low, 0.0)))
        gx[place, pl.ds(TOK, EXTRA)] = ride.astype(BF)

    def placers(ids, count, placer, picker):
        position = lax.broadcasted_iota(jnp.int32, (TILES, CAP), 0)
        slot = lax.broadcasted_iota(jnp.int32, (TILES, CAP), 1)
        held = (position == ids[...]) & (slot < count[...])
        placer[...] = held.astype(F32).astype(BF)
        across = lax.broadcasted_iota(jnp.int32, (CAP, CAP), 0) == lax.broadcasted_iota(jnp.int32, (CAP, CAP), 1)
        picker[...] = dot(across.astype(F32).astype(BF), placer[...], NT).astype(BF)

    def spread(tiles, placer, first, last):
        @pl.loop(first, last, unroll=2)
        def _(k):
            cols = pl.ds(pl.multiple_of(k * 256, 256), 256)
            for upper in range(0, TILES, 256):
                placed = dot(placer[pl.ds(upper, 256), :], tiles[:, cols])
                for row in range(0, 256, 8):
                    for side in range(2):
                        at = (upper + row) * PITCH + 2 * k + side
                        dense[pl.ds(at, 8, stride=PITCH), :] = placed[row : row + 8, side * HEAD : (side + 1) * HEAD]

    def gather_back(tiles, picker, first, last):
        @pl.loop(first, last, unroll=2)
        def _(k):
            cols = pl.ds(pl.multiple_of(k * 256, 256), 256)
            sides = [
                jnp.concatenate(
                    [dense[pl.ds(row * PITCH + 2 * k + side, 8, stride=PITCH), :] for row in range(0, TILES, 8)], axis=0
                ).astype(BF)
                for side in range(2)
            ]
            tiles[:, cols] = dot(picker[...], jnp.concatenate(sides, axis=1)).astype(BF)

    def tile(at):
        return dense[pl.ds(at * PITCH, 32), :]

    def build_out(first, last):
        @pl.loop(first, last, unroll=4)
        def _(g):
            for r in range(4):
                for pair in range(2):
                    at = r * COLS + g * 4 + 2 * pair
                    evens, odds = pair_out(tile(at), tile(at + 1))
                    cols = pl.ds(pair * HEAD, HEAD)
                    w_out[g, pl.ds(r * EDGE, HALF), cols] = evens.astype(BF)
                    w_out[g, pl.ds(r * EDGE + HALF, HALF), cols] = odds.astype(BF)

    def build_val(first, last):
        @pl.loop(first, last, unroll=4)
        def _(g):
            for c in range(4):
                for pair in range(2):
                    at = 2 * pair * COLS + g * 4 + c
                    evens, odds = pair_out(tile(at), tile(at + COLS))
                    cols = pl.ds(pair * HEAD, HEAD)
                    w_val[g, pl.ds(c * EDGE, HALF), cols] = evens.astype(BF)
                    w_val[g, pl.ds(c * EDGE + HALF, HALF), cols] = odds.astype(BF)

    def attention(head):
        cols = pl.ds(head * HEAD, HEAD)
        scores = dot(qin[:, cols], kin[:, cols], NT) * HEAD ** (-0.5)
        scores = jnp.where(rows_at >= cols_at, scores, -1e30)
        weights = jnp.exp(scores - jnp.max(scores, axis=1, keepdims=True))
        probs[head] = (weights / jnp.sum(weights, axis=1, keepdims=True)).astype(BF)
        probs_t[head] = probs[head].T

    def mixed(first, last):
        total = None
        for g in range(first, last):
            term = dot(gu[g], w_out[g], NT)
            total = term if total is None else total + term
        acc[...] = total if first == 0 else acc[...] + total

    def value_grads():
        mixed_grad = dot(acc[...].astype(BF), order, NT).astype(BF)
        for head in range(2):
            cols = pl.ds(head * HEAD, HEAD)
            back = dot(probs_t[head], mixed_grad[:, head * HEAD : (head + 1) * HEAD])
            wide_grads[:, cols] = back
            grads[:, cols] = back.astype(BF)

    def partial_terms(first, last):
        for g in range(first, last):
            part[g] = dot(grads[...], w_val[g], NT).astype(BF)

    def values(first, last):
        total = None
        for g in range(first, last):
            term = dot(gx[g, pl.ds(0, TOK)], w_val[g])
            total = term if total is None else total + term
        acc[...] = total if first == 0 else acc[...] + total

    def attended():
        ride = jnp.zeros((EXTRA, TOK), F32)
        for g in range(BLOCKS):
            ride = ride + gx[g, pl.ds(TOK, EXTRA)].astype(F32)
        flat = jnp.sum(ride, axis=0, keepdims=True)
        squares = jnp.sum(jnp.where(same, flat, 0.0), axis=1, keepdims=True)
        inverse = lax.rsqrt(squares / MODEL + EPS)
        vals[...] = (acc[...] * inverse).astype(BF)
        scaled[...] = (wide_grads[...] * inverse).astype(BF)
        for head in range(2):
            cols = pl.ds(head * HEAD, HEAD)
            grads[:, cols] = dot(probs[head], vals[:, cols]).astype(BF)
        att_t[...] = dot(order, grads[...], (((0,), (1,)), ((), ()))).astype(BF)

    def put(at, value):
        dense[pl.ds(at * PITCH, 32), :] = value

    def full_out(first, last):
        @pl.loop(first, last, unroll=4)
        def _(g):
            block = dot(att_t[...], gu[g])
            for r in range(4):
                for pair in range(2):
                    cols = slice(pair * HEAD, (pair + 1) * HEAD)
                    evens = block[r * EDGE : r * EDGE + HALF, cols]
                    odds = block[r * EDGE + HALF : (r + 1) * EDGE, cols]
                    one, two = pair_out(evens, odds)
                    at = r * COLS + g * 4 + 2 * pair
                    put(at, one)
                    put(at + 1, two)

    def full_val(first, last):
        @pl.loop(first, last, unroll=4)
        def _(g):
            block = dot(gx[g, pl.ds(0, TOK)], scaled[...], TN)
            for c in range(4):
                for pair in range(2):
                    cols = slice(pair * HEAD, (pair + 1) * HEAD)
                    evens = block[c * EDGE : c * EDGE + HALF, cols]
                    odds = block[c * EDGE + HALF : (c + 1) * EDGE, cols]
                    one, two = pair_out(evens, odds)
                    at = 2 * pair * COLS + g * 4 + c
                    put(at, one)
                    put(at + COLS, two)

    def cut(function, parts, total, *given):
        size = total // parts
        return [lambda i=i: function(*given, i * size, (i + 1) * size) for i in range(parts)]

    stores = [
        pltpu.make_async_copy(t_out, out_grad.at[0], load_sems.at[11]),
        pltpu.make_async_copy(t_val, value_grad.at[0], load_sems.at[12]),
    ]

    alone = [
        *(loads[i].wait for i in (7, 8, 9, 10)),
        lambda: placers(out_ids, out_count, place_out, pick_out),
        lambda: placers(val_ids, val_count, place_val, pick_val),
        loads[2].wait,
        *cut(spread, 8, 16, t_out, place_out),
        *cut(build_out, 8, BLOCKS),
        loads[3].wait,
        *cut(spread, 8, 16, t_val, place_val),
        *cut(build_val, 8, BLOCKS),
        loads[4].wait,
        loads[5].wait,
        lambda: attention(0),
        lambda: attention(1),
    ]
    back = [*cut(mixed, 8, BLOCKS), value_grads, *cut(partial_terms, 8, BLOCKS), scatter.begin]
    beside = [
        *cut(values, 8, BLOCKS),
        attended,
        *cut(full_out, 8, BLOCKS),
        *cut(gather_back, 8, 16, t_out, pick_out),
        stores[0].start,
        *cut(full_val, 8, BLOCKS),
        *cut(gather_back, 8, 16, t_val, pick_val),
        stores[1].start,
    ]

    loads[0].wait()
    pl.semaphore_wait(barrier, 6)
    gather_u.begin()
    prepare_x()

    steps_x = [gather_x.begin, *gather_x.steps()]
    early, middle = X_CUTS
    plan = blended(blended(gather_u.steps(), steps_x[:early], X_START), alone, 0.0, 1.0)
    plan += blended(back, steps_x[early:middle])
    sums = scatter.steps()
    plan += blended(sums[:SUMS_FIRST], steps_x[middle:])
    plan += blended(sums[SUMS_FIRST:], beside)
    for step in plan:
        step()

    def finish(rows, total):
        high = total.astype(BF)
        low = (total - high.astype(F32)).astype(BF)
        summed = dot(high, order, NT) + dot(low, order, NT)
        final[pl.ds(*rows)] = (gu[place, pl.ds(*rows)].astype(F32) + summed).astype(BF)

    finish(scatter.b, scatter.lower())
    finish(scatter.a, scatter.upper())

    hand_on = pltpu.make_async_remote_copy(
        src_ref=final,
        dst_ref=passed,
        send_sem=load_sems.at[14],
        recv_sem=load_sems.at[15],
        device_id={"section": before},
        device_id_type=pl.DeviceIdType.MESH,
    )

    @pl.when(section > 0)
    def _():
        hand_on.start()

    @pl.when(section == sections - 1)
    def _():
        passed[...] = jnp.zeros_like(passed)

    for routes in (gather_u, gather_x, scatter):
        routes.sent()

    @pl.when(section < sections - 1)
    def _():
        hand_on.wait_recv()

    last = pltpu.make_async_copy(passed, grad_input.at[0], load_sems.at[13])
    last.start()

    @pl.when(section > 0)
    def _():
        hand_on.wait_send()

    for store in stores:
        store.wait()
    last.wait()


X_CUTS = (9, 16)
X_START = 0.25
SUMS_FIRST = 6
PAIRS = 3 * 38


def backward(x, u, q, k, gain, out_tiles, out_ids, out_count, val_tiles, val_ids, val_count):
    hbm = pl.BlockSpec(memory_space=pltpu.HBM)
    some = pl.BlockSpec(memory_space=pl.ANY)
    rest = TOK - CUT_P
    return pl.pallas_call(
        kernel,
        out_shape=(
            jax.ShapeDtypeStruct((1, TOK, WIDTH), BF),
            jax.ShapeDtypeStruct((1, CAP, EDGE * EDGE), BF),
            jax.ShapeDtypeStruct((1, CAP, EDGE * EDGE), BF),
        ),
        in_specs=[hbm] * 11,
        out_specs=(some, some, some),
        scratch_shapes=[
            pltpu.VMEM((1, CAP), jnp.int32),
            pltpu.VMEM((1, CAP), jnp.int32),
            pltpu.VMEM((1, 1), jnp.int32),
            pltpu.VMEM((1, 1), jnp.int32),
            pltpu.VMEM((1, MODEL), BF),
            pltpu.VMEM((BLOCKS, TOK, WIDTH), BF),
            pltpu.VMEM((BLOCKS, TOK + EXTRA, WIDTH), BF),
            pltpu.VMEM((TOK, WIDTH), BF),
            pltpu.VMEM((TOK, WIDTH), BF),
            pltpu.VMEM((TOK, WIDTH), BF),
            pltpu.VMEM((CAP, EDGE * EDGE), BF),
            pltpu.VMEM((CAP, EDGE * EDGE), BF),
            pltpu.VMEM((TILES, CAP), BF),
            pltpu.VMEM((CAP, TILES), BF),
            pltpu.VMEM((TILES, CAP), BF),
            pltpu.VMEM((CAP, TILES), BF),
            pltpu.VMEM((TILES * PITCH, HEAD), F32),
            pltpu.VMEM((BLOCKS, WIDTH, WIDTH), BF),
            pltpu.VMEM((BLOCKS, WIDTH, WIDTH), BF),
            pltpu.VMEM((2, TOK, TOK), BF),
            pltpu.VMEM((2, TOK, TOK), BF),
            pltpu.VMEM((TOK, WIDTH), F32),
            pltpu.VMEM((TOK, WIDTH), F32),
            pltpu.VMEM((TOK, WIDTH), BF),
            pltpu.VMEM((TOK, WIDTH), BF),
            pltpu.VMEM((TOK, WIDTH), BF),
            pltpu.VMEM((WIDTH, TOK), BF),
            pltpu.VMEM((2, 4, NY, CUT_P, WIDTH), BF),
            pltpu.VMEM((2, 2, NZ, rest, WIDTH), BF),
            pltpu.VMEM((2, 2, CUT_P, WIDTH), BF),
            pltpu.VMEM((2, 4, rest, WIDTH), BF),
            pltpu.VMEM((TOK, WIDTH), BF),
            pltpu.VMEM((TOK, WIDTH), BF),
            pltpu.SemaphoreType.DMA((16,)),
            pltpu.SemaphoreType.DMA((3,)),
            pltpu.SemaphoreType.DMA((PAIRS,)),
        ],
        compiler_params=pltpu.CompilerParams(
            collective_id=0, has_side_effects=True, vmem_limit_bytes=60 * 1024 * 1024
        ),
        cost_estimate=pl.CostEstimate(flops=12 * 2**30, bytes_accessed=12 * 2**20, transcendentals=2**17),
    )(out_ids, val_ids, out_count, val_count, gain, x, u, q, k, out_tiles, val_tiles)


def per_device(
    layer_input, upstream, query_rows, key_rows, norm_gain, out_tiles, out_ids, out_count, value_tiles, value_ids,
    value_count,
):
    return backward(
        layer_input,
        upstream,
        query_rows,
        key_rows,
        norm_gain,
        out_tiles,
        out_ids,
        out_count,
        value_tiles,
        value_ids,
        value_count,
    )


def solution(mesh):
    rows = P("section", None, "tensor")
    tiles = P("section", "tensor", None)
    pair = P("section", "tensor")
    return jax.shard_map(
        per_device,
        mesh=mesh,
        in_specs=(rows, rows, rows, rows, P("section", None), tiles, pair, pair, tiles, pair, pair),
        out_specs=(rows, tiles, tiles),
        check_vma=False,
    )
```

```python
import jax
import jax.numpy as jnp
from jax import lax
from jax.experimental import pallas as pl
from jax.experimental.pallas import tpu as pltpu
from jax.sharding import PartitionSpec as P

HEAD = 128
EDGE = 64
EPS = 1e-05
TOK = 256
WIDTH = 256
NZ = 8
NY = 4
CAP = 320
TILES = 512
COLS = 128
MODEL = 8192
HALF = EDGE // 2
CUT_U, CUT_X, CUT_P = 112, 112, 96
EXTRA = 16
BLOCKS = NZ * NY
PITCH = 33

BF = jnp.bfloat16
F32 = jnp.float32
NN = (((1,), (0,)), ((), ()))
NT = (((1,), (1,)), ((), ()))
TN = (((0,), (0,)), ((), ()))


def dot(a, b, dims=NN):
    return lax.dot_general(a, b, dims, preferred_element_type=F32)


class Links:
    def __init__(self, recv_sems):
        self.recv_sems = recv_sems
        self.used = 0
        place = lax.axis_index("tensor")
        self.place = place
        self.z, self.y = place // NY, place % NY
        self.to = {
            ("z", 1): self.at(1, 0),
            ("z", -1): self.at(-1, 0),
            ("y", 1): self.at(0, 1),
            ("y", -1): self.at(0, -1),
            ("y", 2): self.at(0, 2),
        }

    def at(self, dz, dy):
        return (self.z + (dz + NZ)) % NZ * NY + (self.y + (dy + NY)) % NY

    def semaphore(self):
        self.used += 1
        return self.recv_sems.at[self.used - 1]

    def send(self, src, dst, axis, way, send_sem, recv_sem):
        pltpu.make_async_remote_copy(
            src_ref=src,
            dst_ref=dst,
            send_sem=send_sem,
            recv_sem=recv_sem,
            device_id={"tensor": self.to[(axis, way)]},
            device_id_type=pl.DeviceIdType.MESH,
        ).start()


def wait_for(view, semaphore):
    pltpu.make_async_copy(view, view, semaphore).wait()


WAYS = (1, -1)


class Routes:
    def __init__(self, links, ref, rows, cut, send_sem):
        self.links, self.ref, self.send_sem = links, ref, send_sem
        self.a = (0, cut)
        first = cut // 32 * 16
        self.a_half = {1: (0, first), -1: (first, cut - first)}
        rest = rows - cut
        first = rest // 32 * 16
        self.b = (cut, rest)
        self.b_half = {1: (cut, first), -1: (cut + first, rest - first)}
        self.coming = {}

    def pair(self, key, axis, block, rows, halves, into=None):
        semaphore = self.links.semaphore()
        for way in WAYS:
            part = halves[way] if halves else rows
            src = self.ref.at[block(way), pl.ds(*part)]
            dst = src if into is None else into(way, part[1])
            self.links.send(src, dst, axis, way, self.send_sem, semaphore)
        if halves:
            view = self.ref.at[0, pl.ds(0, rows[1])]
        else:
            view = self.ref.at[pl.ds(0, 2), pl.ds(0, rows[1])]
        self.coming[key] = (view, semaphore)

    def across(self, src, dst):
        semaphore = self.links.semaphore()
        self.links.send(src, dst, "y", 2, self.send_sem, semaphore)
        self.coming[("ay", 2)] = (self.ref.at[0, pl.ds(*self.a)], semaphore)

    def wait(self, *key):
        wait_for(*self.coming.pop(key))

    def sent(self):
        wait_for(self.ref.at[pl.ds(0, BLOCKS - 1)], self.send_sem)


class Gather(Routes):
    def ay(self):
        place = self.links.place
        self.pair(("ay", 1), "y", lambda way: place, self.a, None)
        part = self.ref.at[place, pl.ds(*self.a)]
        self.across(part, part)

    def az(self, step, *offsets):
        at = self.links.at
        for dy in offsets:
            if step > 1:
                self.wait("az", dy, step - 1)
            elif dy == 2:
                self.wait("ay", 2)
            elif dy in (1, -1) and ("ay", 1) in self.coming:
                self.wait("ay", 1)
            self.pair(
                ("az", dy, step),
                "z",
                lambda way: at(-way * (step - 1), dy),
                self.a,
                self.a_half if step == 4 else None,
            )

    def bz(self, step):
        at = self.links.at
        if step > 1:
            self.wait("bz", step - 1)
        self.pair(
            ("bz", step),
            "z",
            lambda way: at(-way * (step - 1), 0),
            self.b,
            self.b_half if step == 4 else None,
        )

    def by1(self, *offsets):
        at = self.links.at
        for dz in offsets:
            if dz == 4:
                self.wait("bz", 4)
            self.pair(("by", dz, 1), "y", lambda way: at(dz, 0), self.b, None)

    def by2(self, *offsets):
        at = self.links.at
        for dz in offsets:
            self.wait("by", dz, 1)
            self.pair(("by", dz, 2), "y", lambda way: at(dz, -way), self.b, self.b_half)

    def moves(self):
        return {"ay": self.ay, "az": self.az, "bz": self.bz, "by1": self.by1, "by2": self.by2, "finish": self.finish}

    def finish(self):
        for key in sorted(self.coming):
            self.wait(*key)


class Scatter(Routes):
    def __init__(self, links, ref, cut, send_sem, az_in, by_in, ay_in, bz_in):
        super().__init__(links, ref, TOK, cut, send_sem)
        self.az_in, self.by_in, self.ay_in, self.bz_in = az_in, by_in, ay_in, bz_in

    def add(self, block, rows, *got):
        part = self.ref[block, pl.ds(*rows)].astype(F32)
        for more in got:
            part = part + more.astype(F32)
        self.ref[block, pl.ds(*rows)] = part.astype(BF)

    def az(self, step, *offsets):
        at = self.links.at
        for dy in offsets:
            if step > 1:
                self.wait("az", dy, step - 1)
                for way in WAYS:
                    rows = self.a if step > 2 else self.a_half[way]
                    got = self.az_in[(way + 1) // 2, step - 2, dy + 1, pl.ds(0, rows[1])]
                    self.add(at(way * (5 - step), dy), rows, got)
            self.pair(
                ("az", dy, step),
                "z",
                lambda way: at(way * (5 - step), dy),
                self.a,
                self.a_half if step == 1 else None,
                lambda way, size: self.az_in.at[(way + 1) // 2, step - 1, dy + 1, pl.ds(0, size)],
            )

    def az_done(self, *offsets):
        for dy in offsets:
            self.wait("az", dy, 4)
            self.add(self.links.at(0, dy), self.a, self.az_in[0, 3, dy + 1], self.az_in[1, 3, dy + 1])

    def by(self, step, *offsets):
        at = self.links.at
        for dz in offsets:
            if step > 1:
                self.wait("by", dz, 1)
                for way in WAYS:
                    rows = self.b_half[way]
                    got = self.by_in[(way + 1) // 2, 0, dz + 3, pl.ds(0, rows[1])]
                    self.add(at(dz, way), rows, got)
            self.pair(
                ("by", dz, step),
                "y",
                lambda way: at(dz, way * (3 - step)),
                self.b,
                self.b_half if step == 1 else None,
                lambda way, size: self.by_in.at[(way + 1) // 2, step - 1, dz + 3, pl.ds(0, size)],
            )

    def by_done(self, *offsets):
        for dz in offsets:
            self.wait("by", dz, 2)
            self.add(self.links.at(dz, 0), self.b, self.by_in[0, 1, dz + 3], self.by_in[1, 1, dz + 3])

    def ay(self):
        at = self.links.at
        self.pair(
            ("ay", 1),
            "y",
            lambda way: at(0, way),
            self.a,
            None,
            lambda way, size: self.ay_in.at[(way + 1) // 2, pl.ds(0, size)],
        )

    def ay_across(self):
        self.across(self.ref.at[self.links.at(0, 2), pl.ds(*self.a)], self.ay_in.at[2])

    def bz(self, step):
        at = self.links.at
        if step > 1:
            self.wait("bz", step - 1)
            for way in WAYS:
                rows = self.b if step > 2 else self.b_half[way]
                got = self.bz_in[(way + 1) // 2, step - 2, pl.ds(0, rows[1])]
                self.add(at(way * (5 - step), 0), rows, got)
        self.pair(
            ("bz", step),
            "z",
            lambda way: at(way * (5 - step), 0),
            self.b,
            self.b_half if step == 1 else None,
            lambda way, size: self.bz_in.at[(way + 1) // 2, step - 1, pl.ds(0, size)],
        )

    def moves(self):
        return {
            "az": self.az,
            "az_done": self.az_done,
            "by": self.by,
            "by_done": self.by_done,
            "bz": self.bz,
            "ay": self.ay,
            "ay_across": self.ay_across,
        }

    def upper(self):
        self.wait("ay", 1)
        self.wait("ay", 2)
        total = self.ref[self.links.place, pl.ds(*self.a)].astype(F32)
        for way in range(3):
            total = total + self.ay_in[way].astype(F32)
        return total

    def lower(self):
        self.wait("bz", 4)
        total = self.ref[self.links.place, pl.ds(*self.b)].astype(F32)
        return total + self.bz_in[0, 3].astype(F32) + self.bz_in[1, 3].astype(F32)


def kernel(
    out_ids_hbm, val_ids_hbm, out_count_hbm, val_count_hbm, gain_hbm, x_hbm, u_hbm, q_hbm, k_hbm, out_hbm, val_hbm,
    grad_input, out_grad, value_grad,
    out_ids, val_ids, out_count, val_count, gain, gu, gx, xin, qin, kin, t_out, t_val, place_out, pick_out, place_val, pick_val, dense, w_out, w_val, probs, probs_t,
    acc, wide_grads, vals, grads, scaled, att_t, az_in, by_in, ay_in, bz_in, final, passed,
    load_sems, send_sems, recv_sems,
):
    links = Links(recv_sems)
    part = w_out
    place = links.place
    section = lax.axis_index("section")
    sections = lax.axis_size("section")
    before, after = (section + sections - 1) % sections, (section + 1) % sections

    loads = [
        pltpu.make_async_copy(src, dst, load_sems.at[i])
        for i, (src, dst) in enumerate(
            (
                (u_hbm.at[0], gu.at[place]),
                (x_hbm.at[0], xin),
                (out_hbm.at[0], t_out),
                (val_hbm.at[0], t_val),
                (q_hbm.at[0], qin),
                (k_hbm.at[0], kin),
                (gain_hbm, gain),
                (out_ids_hbm, out_ids),
                (val_ids_hbm, val_ids),
                (out_count_hbm, out_count),
                (val_count_hbm, val_count),
            )
        )
    ]
    for load in loads:
        load.start()

    barrier = pltpu.get_barrier_semaphore()
    for to in links.to.values():
        pl.semaphore_signal(
            barrier, inc=1, device_id={"tensor": to}, device_id_type=pl.DeviceIdType.MESH
        )
    for to in (before, after):
        pl.semaphore_signal(
            barrier, inc=1, device_id={"section": to}, device_id_type=pl.DeviceIdType.MESH
        )

    gather_u = Gather(links, gu, TOK, CUT_U, send_sems.at[0])
    gather_x = Gather(links, gx, TOK + EXTRA, CUT_X, send_sems.at[1])
    scatter = Scatter(links, part, CUT_P, send_sems.at[2], az_in, by_in, ay_in, bz_in)

    lane = lax.broadcasted_iota(jnp.int32, (HALF, HEAD), 1)
    left = lane < EDGE
    rows_at = lax.broadcasted_iota(jnp.int32, (WIDTH, WIDTH), 0)
    cols_at = lax.broadcasted_iota(jnp.int32, (WIDTH, WIDTH), 1)
    inner = cols_at % EDGE
    natural = cols_at - inner + 2 * (inner % HALF) + inner // HALF
    order = (rows_at == natural).astype(F32).astype(BF)
    same = rows_at == cols_at

    def pair_out(first, second):
        evens = jnp.where(left, first, pltpu.roll(second, EDGE, 1))
        odds = jnp.where(left, pltpu.roll(first, EDGE, 1), second)
        return evens, odds

    def prepare_x():
        loads[1].wait()
        loads[6].wait()
        x = xin[...].astype(F32)
        row = pl.multiple_of(place * WIDTH, WIDTH)
        scaled_x = (x * gain[0:1, pl.ds(row, WIDTH)].astype(F32)).astype(BF)
        gx[place, pl.ds(0, TOK)] = dot(scaled_x, order).astype(BF)
        squares = jnp.sum(x * x, axis=1, keepdims=True)
        flat = jnp.sum(jnp.where(same, squares, 0.0), axis=0, keepdims=True)
        high = flat.astype(BF).astype(F32)
        middle = (flat - high).astype(BF).astype(F32)
        low = flat - high - middle
        at_row = lax.broadcasted_iota(jnp.int32, (EXTRA, TOK), 0)
        ride = jnp.where(at_row == 0, high, jnp.where(at_row == 1, middle, jnp.where(at_row == 2, low, 0.0)))
        gx[place, pl.ds(TOK, EXTRA)] = ride.astype(BF)

    def placers(ids, count, placer, picker):
        position = lax.broadcasted_iota(jnp.int32, (TILES, CAP), 0)
        slot = lax.broadcasted_iota(jnp.int32, (TILES, CAP), 1)
        held = (position == ids[...]) & (slot < count[...])
        placer[...] = held.astype(F32).astype(BF)
        across = lax.broadcasted_iota(jnp.int32, (CAP, CAP), 0) == lax.broadcasted_iota(jnp.int32, (CAP, CAP), 1)
        picker[...] = dot(across.astype(F32).astype(BF), placer[...], NT).astype(BF)

    def spread(tiles, placer, first, last):
        @pl.loop(first, last, unroll=2)
        def _(k):
            cols = pl.ds(pl.multiple_of(k * 256, 256), 256)
            for upper in range(0, TILES, 256):
                placed = dot(placer[pl.ds(upper, 256), :], tiles[:, cols])
                for row in range(0, 256, 8):
                    for side in range(2):
                        at = (upper + row) * PITCH + 2 * k + side
                        dense[pl.ds(at, 8, stride=PITCH), :] = placed[row : row + 8, side * HEAD : (side + 1) * HEAD]

    def gather_back(tiles, picker, first, last):
        @pl.loop(first, last, unroll=2)
        def _(k):
            cols = pl.ds(pl.multiple_of(k * 256, 256), 256)
            sides = [
                jnp.concatenate(
                    [dense[pl.ds(row * PITCH + 2 * k + side, 8, stride=PITCH), :] for row in range(0, TILES, 8)], axis=0
                ).astype(BF)
                for side in range(2)
            ]
            tiles[:, cols] = dot(picker[...], jnp.concatenate(sides, axis=1)).astype(BF)

    def tile(at):
        return dense[pl.ds(at * PITCH, 32), :]

    def build_out(first, last):
        @pl.loop(first, last, unroll=4)
        def _(g):
            for r in range(4):
                for pair in range(2):
                    at = r * COLS + g * 4 + 2 * pair
                    evens, odds = pair_out(tile(at), tile(at + 1))
                    cols = pl.ds(pair * HEAD, HEAD)
                    w_out[g, pl.ds(r * EDGE, HALF), cols] = evens.astype(BF)
                    w_out[g, pl.ds(r * EDGE + HALF, HALF), cols] = odds.astype(BF)

    def build_val(first, last):
        @pl.loop(first, last, unroll=4)
        def _(g):
            for c in range(4):
                for pair in range(2):
                    at = 2 * pair * COLS + g * 4 + c
                    evens, odds = pair_out(tile(at), tile(at + COLS))
                    cols = pl.ds(pair * HEAD, HEAD)
                    w_val[g, pl.ds(c * EDGE, HALF), cols] = evens.astype(BF)
                    w_val[g, pl.ds(c * EDGE + HALF, HALF), cols] = odds.astype(BF)

    def attention(head):
        cols = pl.ds(head * HEAD, HEAD)
        scores = dot(qin[:, cols], kin[:, cols], NT) * HEAD ** (-0.5)
        scores = jnp.where(rows_at >= cols_at, scores, -1e30)
        weights = jnp.exp(scores - jnp.max(scores, axis=1, keepdims=True))
        probs[head] = (weights / jnp.sum(weights, axis=1, keepdims=True)).astype(BF)
        probs_t[head] = probs[head].T

    def mixed(first, last):
        total = None
        for g in range(first, last):
            term = dot(gu[g], w_out[g], NT)
            total = term if total is None else total + term
        acc[...] = total if first == 0 else acc[...] + total

    def value_grads():
        mixed_grad = dot(acc[...].astype(BF), order, NT).astype(BF)
        for head in range(2):
            cols = pl.ds(head * HEAD, HEAD)
            back = dot(probs_t[head], mixed_grad[:, head * HEAD : (head + 1) * HEAD])
            wide_grads[:, cols] = back
            grads[:, cols] = back.astype(BF)

    def partial_terms(first, last):
        for g in range(first, last):
            part[g] = dot(grads[...], w_val[g], NT).astype(BF)

    def values(first, last):
        total = None
        for g in range(first, last):
            term = dot(gx[g, pl.ds(0, TOK)], w_val[g])
            total = term if total is None else total + term
        acc[...] = total if first == 0 else acc[...] + total

    def attended():
        ride = jnp.zeros((EXTRA, TOK), F32)
        for g in range(BLOCKS):
            ride = ride + gx[g, pl.ds(TOK, EXTRA)].astype(F32)
        flat = jnp.sum(ride, axis=0, keepdims=True)
        squares = jnp.sum(jnp.where(same, flat, 0.0), axis=1, keepdims=True)
        inverse = lax.rsqrt(squares / MODEL + EPS)
        vals[...] = (acc[...] * inverse).astype(BF)
        scaled[...] = (wide_grads[...] * inverse).astype(BF)
        for head in range(2):
            cols = pl.ds(head * HEAD, HEAD)
            grads[:, cols] = dot(probs[head], vals[:, cols]).astype(BF)
        att_t[...] = dot(order, grads[...], (((0,), (1,)), ((), ()))).astype(BF)

    def put(at, value):
        dense[pl.ds(at * PITCH, 32), :] = value

    def full_out(first, last):
        @pl.loop(first, last, unroll=4)
        def _(g):
            block = dot(att_t[...], gu[g])
            for r in range(4):
                for pair in range(2):
                    cols = slice(pair * HEAD, (pair + 1) * HEAD)
                    evens = block[r * EDGE : r * EDGE + HALF, cols]
                    odds = block[r * EDGE + HALF : (r + 1) * EDGE, cols]
                    one, two = pair_out(evens, odds)
                    at = r * COLS + g * 4 + 2 * pair
                    put(at, one)
                    put(at + 1, two)

    def full_val(first, last):
        @pl.loop(first, last, unroll=4)
        def _(g):
            block = dot(gx[g, pl.ds(0, TOK)], scaled[...], TN)
            for c in range(4):
                for pair in range(2):
                    cols = slice(pair * HEAD, (pair + 1) * HEAD)
                    evens = block[c * EDGE : c * EDGE + HALF, cols]
                    odds = block[c * EDGE + HALF : (c + 1) * EDGE, cols]
                    one, two = pair_out(evens, odds)
                    at = 2 * pair * COLS + g * 4 + c
                    put(at, one)
                    put(at + COLS, two)

    def cut(function, parts, total, *given):
        size = total // parts
        return [lambda i=i: function(*given, i * size, (i + 1) * size) for i in range(parts)]

    stores = [
        pltpu.make_async_copy(t_out, out_grad.at[0], load_sems.at[11]),
        pltpu.make_async_copy(t_val, value_grad.at[0], load_sems.at[12]),
    ]

    alone = [
        lambda: ([loads[i].wait() for i in (7, 8, 9, 10)], placers(out_ids, out_count, place_out, pick_out)),
        lambda: placers(val_ids, val_count, place_val, pick_val),
        lambda: (loads[2].wait(), spread(t_out, place_out, 0, 2)),
        *cut(spread, 8, 16, t_out, place_out)[1:],
        *cut(build_out, 8, BLOCKS),
        lambda: (loads[3].wait(), spread(t_val, place_val, 0, 2)),
        *cut(spread, 8, 16, t_val, place_val)[1:],
        *cut(build_val, 8, BLOCKS),
        lambda: (loads[4].wait(), loads[5].wait(), attention(0)),
        lambda: attention(1),
    ]
    back = [*cut(mixed, 8, BLOCKS), value_grads, *cut(partial_terms, 8, BLOCKS)]
    beside = [
        *cut(values, 8, BLOCKS),
        attended,
        *cut(full_out, 8, BLOCKS),
        *cut(gather_back, 8, 16, t_out, pick_out)[:-1],
        lambda: (gather_back(t_out, pick_out, 14, 16), stores[0].start()),
        *cut(full_val, 8, BLOCKS),
        *cut(gather_back, 8, 16, t_val, pick_val)[:-1],
        lambda: (gather_back(t_val, pick_val, 14, 16), stores[1].start()),
    ]

    loads[0].wait()
    pl.semaphore_wait(barrier, 7)

    compute = {"alone": iter(alone), "back": iter(back), "beside": iter(beside)}
    routes_of = {"u": gather_u, "x": gather_x, "p": scatter}
    prepared = False
    for where, what, *given in PLAN:
        if where == "c":
            next(compute[what])()
            continue
        if where == "x" and not prepared:
            prepare_x()
            prepared = True
        moves = routes_of[where].moves()
        moves[what](*given)
    for rest in compute.values():
        for step in rest:
            step()

    def finish(rows, total):
        high = total.astype(BF)
        low = (total - high.astype(F32)).astype(BF)
        summed = dot(high, order, NT) + dot(low, order, NT)
        final[pl.ds(*rows)] = (gu[place, pl.ds(*rows)].astype(F32) + summed).astype(BF)

    halves = []
    for i, (rows, total) in enumerate(((scatter.b, scatter.lower), (scatter.a, scatter.upper))):
        finish(rows, total())
        hand_on = pltpu.make_async_remote_copy(
            src_ref=final.at[pl.ds(*rows)],
            dst_ref=passed.at[pl.ds(*rows)],
            send_sem=load_sems.at[14 + i],
            recv_sem=load_sems.at[16 + i],
            device_id={"section": before},
            device_id_type=pl.DeviceIdType.MESH,
        )
        halves.append(hand_on)
        pl.when(section > 0)(hand_on.start)

    @pl.when(section == sections - 1)
    def _():
        passed[...] = jnp.zeros_like(passed)

    for routes in (gather_u, gather_x, scatter):
        routes.sent()

    for hand_on in halves:
        pl.when(section < sections - 1)(hand_on.wait_recv)

    last = pltpu.make_async_copy(passed, grad_input.at[0], load_sems.at[13])
    last.start()

    for hand_on in halves:
        pl.when(section > 0)(hand_on.wait_send)

    for store in stores:
        store.wait()
    last.wait()


PLAN = (
    ("u", "ay"), ("u", "bz", 1), ("u", "az", 1, 0), ("u", "by1", 0), ("c", "alone"), ("c", "alone"), ("c", "alone"),
    ("c", "alone"), ("c", "alone"), ("x", "bz", 1), ("c", "alone"), ("c", "alone"), ("c", "alone"), ("c", "alone"),
    ("x", "ay"), ("c", "alone"), ("c", "alone"), ("u", "az", 1, 1), ("u", "az", 1, -1), ("c", "alone"),
    ("c", "alone"), ("u", "bz", 2), ("u", "by1", 1), ("u", "by1", -1), ("c", "alone"), ("c", "alone"),
    ("c", "alone"), ("c", "alone"), ("u", "az", 1, 2), ("c", "alone"), ("c", "alone"), ("u", "az", 2, 0),
    ("c", "alone"), ("c", "alone"), ("c", "alone"), ("c", "alone"), ("u", "by2", 0), ("c", "alone"), ("c", "alone"),
    ("c", "alone"), ("c", "alone"), ("c", "alone"), ("c", "alone"), ("c", "alone"), ("c", "alone"), ("c", "alone"),
    ("u", "az", 2, 1), ("c", "alone"), ("c", "alone"), ("c", "alone"), ("c", "alone"), ("u", "az", 2, -1),
    ("x", "by1", 0), ("u", "by2", 1), ("u", "bz", 3), ("u", "by1", -2), ("u", "by1", 2), ("u", "by2", -1),
    ("u", "az", 2, 2), ("u", "az", 3, 0), ("u", "az", 3, 1), ("u", "az", 3, -1), ("x", "by2", 0), ("u", "by2", -2),
    ("u", "bz", 4), ("u", "by1", 3), ("u", "by1", -3), ("u", "by2", 2), ("u", "az", 3, 2), ("u", "az", 4, 0),
    ("u", "az", 4, 1), ("u", "az", 4, -1), ("u", "by2", 3), ("x", "bz", 2), ("x", "by1", -1), ("u", "by1", 4),
    ("u", "by2", -3), ("u", "az", 4, 2), ("x", "az", 1, 1), ("x", "by1", 1), ("x", "az", 1, -1), ("x", "az", 1, 0),
    ("x", "by2", -1), ("u", "by2", 4), ("x", "bz", 3), ("x", "by1", 2), ("x", "az", 2, 1), ("x", "by2", 1),
    ("x", "az", 2, -1), ("x", "by1", -2), ("u", "finish"), ("c", "back"), ("x", "az", 1, 2), ("c", "back"),
    ("c", "back"), ("x", "bz", 4), ("c", "back"), ("x", "by1", 3), ("c", "back"), ("x", "az", 3, 1), ("c", "back"),
    ("c", "back"), ("x", "by2", 2), ("c", "back"), ("x", "az", 2, 0), ("c", "back"), ("x", "by2", -2), ("c", "back"),
    ("x", "az", 2, 2), ("c", "back"), ("x", "by1", -3), ("c", "back"), ("c", "back"), ("c", "back"), ("c", "back"),
    ("c", "back"), ("x", "az", 3, -1), ("c", "back"), ("x", "by1", 4), ("x", "az", 4, 1), ("p", "az", 1, -1),
    ("x", "by2", 3), ("x", "az", 3, 0), ("p", "by", 1, 4), ("x", "az", 3, 2), ("x", "by2", -3), ("x", "az", 4, -1),
    ("p", "by", 1, -3), ("p", "az", 1, 1), ("x", "by2", 4), ("p", "az", 1, 0), ("p", "az", 1, 2), ("p", "by", 1, 3),
    ("x", "az", 4, 0), ("p", "by", 2, 4), ("p", "az", 2, -1), ("x", "az", 4, 2), ("p", "az", 2, 1),
    ("p", "by", 2, -3), ("p", "az", 2, 2), ("p", "by", 1, 2), ("p", "az", 2, 0), ("p", "by", 2, 3), ("x", "finish"),
    ("p", "by_done", 4), ("p", "az", 3, -1), ("c", "beside"), ("c", "beside"), ("c", "beside"), ("p", "bz", 1),
    ("p", "by", 1, -2), ("c", "beside"), ("p", "by_done", -3), ("p", "az", 3, 1), ("p", "by", 1, 1), ("c", "beside"),
    ("c", "beside"), ("c", "beside"), ("p", "az", 3, 2), ("p", "by", 2, 2), ("c", "beside"), ("c", "beside"),
    ("p", "by_done", 3), ("p", "az", 4, -1), ("p", "by", 1, -1), ("c", "beside"), ("p", "bz", 2), ("p", "by", 2, -2),
    ("c", "beside"), ("c", "beside"), ("c", "beside"), ("c", "beside"), ("c", "beside"), ("c", "beside"),
    ("p", "az", 3, 0), ("c", "beside"), ("p", "by", 2, 1), ("c", "beside"), ("p", "by_done", 2), ("p", "az", 4, 1),
    ("p", "az_done", -1), ("c", "beside"), ("c", "beside"), ("p", "az", 4, 2), ("p", "by", 2, -1), ("c", "beside"),
    ("c", "beside"), ("c", "beside"), ("p", "by_done", -2), ("p", "bz", 3), ("p", "by", 1, 0), ("c", "beside"),
    ("c", "beside"), ("c", "beside"), ("c", "beside"), ("p", "az", 4, 0), ("p", "az_done", 1), ("p", "ay"),
    ("p", "by_done", 1), ("c", "beside"), ("p", "az_done", 2), ("p", "ay_across"), ("c", "beside"),
    ("p", "by_done", -1), ("c", "beside"), ("c", "beside"), ("c", "beside"), ("p", "by", 2, 0), ("p", "bz", 4),
    ("c", "beside"), ("c", "beside"), ("c", "beside"), ("c", "beside"), ("p", "az_done", 0), ("c", "beside"),
    ("c", "beside"), ("c", "beside"), ("c", "beside"), ("c", "beside"), ("p", "by_done", 0),
)
PAIRS = 3 * 38


def backward(x, u, q, k, gain, out_tiles, out_ids, out_count, val_tiles, val_ids, val_count):
    hbm = pl.BlockSpec(memory_space=pltpu.HBM)
    some = pl.BlockSpec(memory_space=pl.ANY)
    rest = TOK - CUT_P
    return pl.pallas_call(
        kernel,
        out_shape=(
            jax.ShapeDtypeStruct((1, TOK, WIDTH), BF),
            jax.ShapeDtypeStruct((1, CAP, EDGE * EDGE), BF),
            jax.ShapeDtypeStruct((1, CAP, EDGE * EDGE), BF),
        ),
        in_specs=[hbm] * 11,
        out_specs=(some, some, some),
        scratch_shapes=[
            pltpu.VMEM((1, CAP), jnp.int32),
            pltpu.VMEM((1, CAP), jnp.int32),
            pltpu.VMEM((1, 1), jnp.int32),
            pltpu.VMEM((1, 1), jnp.int32),
            pltpu.VMEM((1, MODEL), BF),
            pltpu.VMEM((BLOCKS, TOK, WIDTH), BF),
            pltpu.VMEM((BLOCKS, TOK + EXTRA, WIDTH), BF),
            pltpu.VMEM((TOK, WIDTH), BF),
            pltpu.VMEM((TOK, WIDTH), BF),
            pltpu.VMEM((TOK, WIDTH), BF),
            pltpu.VMEM((CAP, EDGE * EDGE), BF),
            pltpu.VMEM((CAP, EDGE * EDGE), BF),
            pltpu.VMEM((TILES, CAP), BF),
            pltpu.VMEM((CAP, TILES), BF),
            pltpu.VMEM((TILES, CAP), BF),
            pltpu.VMEM((CAP, TILES), BF),
            pltpu.VMEM((TILES * PITCH, HEAD), F32),
            pltpu.VMEM((BLOCKS, WIDTH, WIDTH), BF),
            pltpu.VMEM((BLOCKS, WIDTH, WIDTH), BF),
            pltpu.VMEM((2, TOK, TOK), BF),
            pltpu.VMEM((2, TOK, TOK), BF),
            pltpu.VMEM((TOK, WIDTH), F32),
            pltpu.VMEM((TOK, WIDTH), F32),
            pltpu.VMEM((TOK, WIDTH), BF),
            pltpu.VMEM((TOK, WIDTH), BF),
            pltpu.VMEM((TOK, WIDTH), BF),
            pltpu.VMEM((WIDTH, TOK), BF),
            pltpu.VMEM((2, 4, NY, CUT_P, WIDTH), BF),
            pltpu.VMEM((2, 2, NZ, rest, WIDTH), BF),
            pltpu.VMEM((3, CUT_P, WIDTH), BF),
            pltpu.VMEM((2, 4, rest, WIDTH), BF),
            pltpu.VMEM((TOK, WIDTH), BF),
            pltpu.VMEM((TOK, WIDTH), BF),
            pltpu.SemaphoreType.DMA((18,)),
            pltpu.SemaphoreType.DMA((3,)),
            pltpu.SemaphoreType.DMA((PAIRS,)),
        ],
        compiler_params=pltpu.CompilerParams(
            collective_id=0, has_side_effects=True, vmem_limit_bytes=60 * 1024 * 1024
        ),
        cost_estimate=pl.CostEstimate(flops=12 * 2**30, bytes_accessed=12 * 2**20, transcendentals=2**17),
    )(out_ids, val_ids, out_count, val_count, gain, x, u, q, k, out_tiles, val_tiles)


def per_device(
    layer_input, upstream, query_rows, key_rows, norm_gain, out_tiles, out_ids, out_count, value_tiles, value_ids,
    value_count,
):
    return backward(
        layer_input,
        upstream,
        query_rows,
        key_rows,
        norm_gain,
        out_tiles,
        out_ids,
        out_count,
        value_tiles,
        value_ids,
        value_count,
    )


def solution(mesh):
    rows = P("section", None, "tensor")
    tiles = P("section", "tensor", None)
    pair = P("section", "tensor")
    return jax.shard_map(
        per_device,
        mesh=mesh,
        in_specs=(rows, rows, rows, rows, P("section", None), tiles, pair, pair, tiles, pair, pair),
        out_specs=(rows, tiles, tiles),
        check_vma=False,
    )
```
